32 devices in a mesh: grp: 2 (over y), tok: 4 (over z), blk: 4 (over x, core).
Axes of the slice: x: 2, y: 2, z: 4, core: 2. Of those that a mesh axis runs over, the one named last changes fastest.
Arguments:
- student: bfloat16 [16384, 2048], P(('grp', 'tok', 'blk')), parts along dimension 0, may hold values from -6 to 6
- teacher: bfloat16 [512, 2048], P(('grp', 'blk'), 'tok'), parts along dimension 0, may hold values from -6 to 6
- student_mask: int32 [16384], P(('grp', 'tok', 'blk')), parts along dimension 0, may hold values from 0 to 1, as said below
- teacher_mask: int32 [512], P(('grp', 'blk')), parts along dimension 0, may hold values from 0 to 1, as said below
Outputs:
- targets: bfloat16 [16384, 2048], P(('grp', 'tok', 'blk')), parts along dimension 0
- potential: float32 [16384], P(('grp', 'tok', 'blk')), parts along dimension 0
The draws below stay inside these ranges and needn't reach their ends.
There are 2 independent parts, one for each index of `grp`. The reference program is written for one: setup_inputs(seed, part) draws one part's arguments, and reference() takes and returns one part's arrays. A program takes and returns all parts, laid end to end along the dimension named above; each array names one. Nothing has to cross between parts.
Inputs may be any that keep to these rules, and one draw needn't show every extreme that they name: `student_mask`: each aligned block of 512 positions holds ones on a prefix of 128 to 512 positions and zeros after it; the last block is all ones. `teacher_mask`: each aligned block of 64 positions holds ones on a prefix of 16 to 64 positions and zeros after it; the last block is all ones.
All inputs are finite; a program needn't handle non-finite values.
Results may differ from the reference program's by a relative error of at most 0.0045.
Values may be sent and summed in bfloat16 or wider, within the bound.
A program may use at most 64 MiB of HBM per device.

```python
import math
import jax
import jax.numpy as jnp
from jax import lax

P_SIZE = 2048
NS_DEV = 512
TB = 64
ITERS = 3
N = 8192
M = 256
N_BLK = 4


gap_levels = (6.0, 1.5, 4.5, 3.0)


def shared_rows(key, limit):
    return jax.random.uniform(key, (M // TB, P_SIZE), jnp.float32, -limit, limit)


def drawn_amplitude():
    return min(3.4, 3.55 * (64.0 / P_SIZE) ** 0.25)


def drawn_strength():
    levels = jnp.array([1.75, 1.2, 0.8], jnp.float32)
    return levels[jnp.arange(M // TB) % 3]


def topic_rows(key, factor):
    amplitudes = jnp.array([factor * (0.75 * gap_level / P_SIZE ** 0.5) ** 0.5 for gap_level in gap_levels], jnp.float32)
    vectors = jax.random.uniform(jax.random.fold_in(key, 101), (len(gap_levels), P_SIZE), jnp.float32, -1.0, 1.0)
    return amplitudes[:, None] * vectors


def outlier_channels(key):
    shuffled = jax.random.permutation(jax.random.fold_in(key, 103), P_SIZE)
    chosen = shuffled[:max(P_SIZE // 32, 1)]
    return jnp.zeros((P_SIZE,), jnp.float32).at[chosen].set(1.0)[None, :]


def teacher_topics(key):
    topic_codes = jax.random.randint(jax.random.fold_in(key, 107), (M,), 0, 16)
    return (topic_codes >= 1).astype(jnp.int32) + (topic_codes >= 9).astype(jnp.int32) + (topic_codes >= 12).astype(jnp.int32)


def student_topics(key):
    offset = jax.random.randint(jax.random.fold_in(key, 109), (), 0, len(gap_levels))
    group_ids = jnp.arange(N, dtype=jnp.int32) // (NS_DEV * N_BLK)
    return (group_ids + offset) % len(gap_levels)


def prefix_mask(key, blocks, span):
    lengths = jax.random.randint(key, (blocks,), span // 4, span + 1)
    lengths = lengths.at[blocks - 1].set(span)
    places = jnp.arange(span, dtype=jnp.int32)[None, :]
    return (places < lengths[:, None]).astype(jnp.int32).reshape(blocks * span)


def draw_teacher(key, part):
    common = key
    key = jax.random.fold_in(key, 11)
    amplitude = drawn_amplitude()
    leaders = jnp.arange(M // TB) * TB
    shared = shared_rows(common, amplitude)
    topical = topic_rows(common, 2.0)[teacher_topics(common)]
    channels = outlier_channels(common)
    quiet = 0.1 * jax.random.truncated_normal(jax.random.fold_in(key, 7), -3.0, 3.0, (M, P_SIZE), jnp.float32)
    states = 1.2 * jax.random.truncated_normal(key, -3.5, 3.5, (M, P_SIZE), jnp.float32) + topical
    states = states.at[leaders].set(shared)
    states = jnp.where(channels > 0, quiet, states)
    sink_rows = jnp.where(channels > 0, -6.0, quiet[leaders + 1])
    states = states.at[leaders + 1].set(sink_rows)
    return states.astype(jnp.bfloat16)


def draw_student(key, part):
    common = key
    key = jax.random.fold_in(key, 23)
    amplitude = drawn_amplitude()
    shared = shared_rows(common, amplitude)
    places = jnp.arange(M // TB) * NS_DEV
    planted = drawn_strength()[:, None] * shared
    topical = topic_rows(common, 0.5)[student_topics(common)]
    channels = outlier_channels(common)
    fresh_draw = jax.random.truncated_normal(key, -3.5, 3.5, (N, P_SIZE), jnp.float32)
    states = 0.3 * fresh_draw + topical
    outlier = 5.0 + 0.25 * fresh_draw
    states = states.at[places].set(planted)
    states = jnp.where(channels > 0, outlier, states)
    return states.astype(jnp.bfloat16)


def draw_student_mask(key, part):
    key = jax.random.fold_in(key, 37)
    return prefix_mask(key, N // NS_DEV, NS_DEV)


def draw_teacher_mask(key, part):
    key = jax.random.fold_in(key, 41)
    return prefix_mask(key, M // TB, TB)


def setup_inputs(seed: int = 0, part: int = 0) -> dict:
    splits = jax.random.split(jax.random.key(seed), 5)
    part_splits = jax.random.split(jax.random.fold_in(splits[4], part), 5)
    return {
        "student": draw_student(jax.random.fold_in(jax.random.fold_in(splits[4], part), 71), part),
        "teacher": draw_teacher(jax.random.fold_in(jax.random.fold_in(splits[4], part), 71), part),
        "student_mask": draw_student_mask(jax.random.fold_in(jax.random.fold_in(splits[4], part), 71), part),
        "teacher_mask": draw_teacher_mask(jax.random.fold_in(jax.random.fold_in(splits[4], part), 71), part),
    }


EPS = 0.25
NEG = -1e+30

def log_sum(values, axis):
    top = lax.optimization_barrier(jnp.max(values, axis=axis, keepdims=True))
    total = lax.optimization_barrier(jnp.sum(jnp.exp(values - top), axis=axis))
    return jnp.squeeze(top, axis) + jnp.log(total)

def reference(student, teacher, student_mask, teacher_mask):
    scale = 1.0 / (math.sqrt(student.shape[1]) * EPS)
    scores = jnp.dot(student, teacher.T, preferred_element_type=jnp.float32) * scale
    student_total = jnp.sum(student_mask).astype(jnp.float32)
    teacher_total = jnp.sum(teacher_mask).astype(jnp.float32)
    log_student = jnp.where(student_mask > 0, -jnp.log(student_total), NEG).astype(jnp.float32)
    log_teacher = jnp.where(teacher_mask > 0, -jnp.log(teacher_total), NEG).astype(jnp.float32)
    dual = jnp.zeros((teacher.shape[0],), jnp.float32)
    potential = jnp.zeros((student.shape[0],), jnp.float32)
    for step in range(ITERS):
        potential = -EPS * log_sum(scores + (dual / EPS + log_teacher)[None, :], 1)
        dual = -EPS * log_sum(scores + (potential / EPS + log_student)[:, None], 0)
    exponent = scores + (potential / EPS)[:, None] + (dual / EPS + log_teacher)[None, :]
    weights = jnp.where((student_mask > 0)[:, None], jnp.exp(exponent), 0.0).astype(jnp.bfloat16)
    targets = jnp.dot(weights, teacher, preferred_element_type=jnp.float32).astype(jnp.bfloat16)
    return (targets, potential)
```

```python
import functools
import math

import jax
import jax.numpy as jnp
from jax import lax
from jax.experimental import pallas as pl
from jax.experimental.pallas import tpu as pltpu
from jax.sharding import PartitionSpec as P

ITERS = 3
EPS = 0.25
NEG = -1e30
ROWS = 64
DIRECT = 16


def kernel(
    nt, nb, phases, scale,
    student_hbm, teacher_hbm, student_mask, teacher_mask,
    targets_hbm, potential_ref,
    x_ref, all_t, s_ref, c_ref, lse_ref, o_ref, meta, stats,
    local_sem, out_sem, tok_send, tok_recv, blk_send, blk_recv, meta_send, meta_recv, stat_send, stat_recv,
):
    rows, width = x_ref.shape
    tb, fs = teacher_hbm.shape
    m = nb * tb
    t, b = lax.axis_index("tok"), lax.axis_index("blk")
    bits = [1 << k for k in reversed(range(nb.bit_length() - 1))]

    load_x = pltpu.make_async_copy(student_hbm, x_ref, local_sem.at[0])
    load_x.start()

    def block(c, owner):
        return all_t.at[c, pl.ds(pl.multiple_of(owner * tb, tb), tb), :]

    load_t = pltpu.make_async_copy(teacher_hbm, block(t, b), local_sem.at[1])
    load_t.start()

    def others(axes):
        spans = [range(nt) if "tok" in axes else range(1), range(nb) if "blk" in axes else range(1)]
        return [(i, j) for i in spans[0] for j in spans[1] if i or j]

    def peer(i, j):
        return {"tok": t ^ i, "blk": b ^ j}

    greeted = sorted({p for axes in phases for p in others(axes)} | {p for p in others(("tok",))} | {p for p in others(("blk",))})
    barrier = pltpu.get_barrier_semaphore()
    for i, j in greeted:
        pl.semaphore_signal(barrier, inc=1, device_id=peer(i, j), device_id_type=pl.DeviceIdType.MESH)
    pl.semaphore_wait(barrier, len(greeted))

    def place(axes):
        if len(axes) == 2:
            return t * nb + b
        return t if "tok" in axes else b

    def send_all(ref, send, recv, axes):
        mine = place(axes)
        for i, j in others(axes):
            pltpu.make_async_remote_copy(
                src_ref=ref.at[mine], dst_ref=ref.at[mine], send_sem=send, recv_sem=recv,
                device_id=peer(i, j), device_id_type=pl.DeviceIdType.MESH,
            ).start()

    def wait_bytes(ref, sem):
        pltpu.make_async_copy(ref, ref, sem).wait()

    def arrived(ref, recv, axes):
        wait_bytes(ref.at[pl.ds(0, len(others(axes)))], recv)

    def meta_values():
        ns = jnp.sum(student_mask[...].astype(jnp.float32), axis=1, keepdims=True)
        nteach = jnp.sum(teacher_mask[...].astype(jnp.float32), axis=1, keepdims=True)
        return ns, nteach

    own_students, own_teachers = meta_values()

    def tok_copy(i, source):
        return pltpu.make_async_remote_copy(
            src_ref=teacher_hbm, dst_ref=block(source, b), send_sem=tok_send, recv_sem=tok_recv.at[source],
            device_id=peer(i, 0), device_id_type=pl.DeviceIdType.MESH,
        )

    def blk_copy(c, owner, bit):
        return pltpu.make_async_remote_copy(
            src_ref=block(c, owner), dst_ref=block(c, owner), send_sem=blk_send, recv_sem=blk_recv.at[c, owner],
            device_id=peer(0, bit), device_id_type=pl.DeviceIdType.MESH,
        )

    for i in range(1, nt):
        tok_copy(i, t).start()

    def hold_own(d):
        c = t ^ d
        if isinstance(d, int) and d == 0:
            load_t.wait()
        else:
            tok_copy(0, c).wait_recv()
        for bit in bits:
            blk_copy(c, b, bit).start()

    def forward(d, lowest):
        c = t ^ d
        for h in range(1, nb):
            if (h & -h) != lowest:
                continue
            blk_copy(c, b ^ h, lowest).wait_recv()
            for bit in bits:
                if bit < lowest:
                    blk_copy(c, b ^ h, bit).start()

    hold_own(0)

    meta[0][place(phases[0])] = jnp.concatenate(
        [jnp.broadcast_to(own_students, (1, 128)), jnp.broadcast_to(own_teachers, (1, 128))], axis=1
    )
    send_all(meta[0], meta_send.at[0], meta_recv.at[0], phases[0])

    def multiply(c, columns, first):
        part = lax.dot_general(
            x_ref[:, columns], all_t[c], (((1,), (1,)), ((), ())), preferred_element_type=jnp.float32
        )
        if first:
            s_ref[...] = part
        else:
            s_ref[...] += part

    aligned = fs % 128 == 0 and nt <= 8
    if aligned:
        for d in range(nt + len(bits)):
            if 0 < d < nt:
                hold_own(d)
            for k, bit in enumerate(bits):
                if 0 <= d - k - 1 < nt:
                    forward(d - k - 1, bit)
            done = d - len(bits)
            if 0 <= done < nt:
                if done == 0:
                    load_x.wait()
                c = t ^ done
                multiply(c, pl.ds(pl.multiple_of(c * fs, 128), fs), done == 0)
    else:
        def step(d, carry):
            hold_own(d)
            return carry

        lax.fori_loop(1, nt, step, 0)
        for bit in bits:
            def pass_on(d, carry, bit=bit):
                forward(d, bit)
                return carry

            lax.fori_loop(0, nt, pass_on, 0)
        load_x.wait()
        for c in range(nt):
            multiply(c, pl.ds(c * fs, fs), c == 0)

    arrived(meta[0], meta_recv.at[0], phases[0])
    lane = lax.broadcasted_iota(jnp.int32, (1, m), 1)
    limit = jnp.zeros((1, m), jnp.float32)
    teacher_total = jnp.zeros((1, 1), jnp.float32)
    for j in range(nb):
        slot = t * nb + j if len(phases[0]) == 2 else j
        held = meta[0][slot][:, 128:129]
        teacher_total += held
        limit = jnp.where(lane // tb == j, held, limit)
    valid_teacher = (lane % tb).astype(jnp.float32) < limit
    log_teacher = jnp.where(valid_teacher, -jnp.log(teacher_total), NEG)
    student_total = jnp.sum(meta[0][...][:, :, 0:1], axis=0)
    if len(phases) == 2:
        meta[1][place(phases[1])] = jnp.broadcast_to(student_total, (1, 256))
        send_all(meta[1], meta_send.at[1], meta_recv.at[1], phases[1])
        arrived(meta[1], meta_recv.at[1], phases[1])
        student_total = jnp.sum(meta[1][...][:, :, 0:1], axis=0)
    log_count = jnp.log(student_total)

    def log_sum(values):
        top = jnp.max(values, axis=0)
        return top + jnp.log(jnp.sum(jnp.exp(values - top[None]), axis=0))

    terms = log_teacher
    for it in range(ITERS):
        top = jnp.full((8, m), -jnp.inf, jnp.float32)
        for r in range(0, rows, ROWS):
            s = s_ref[pl.ds(r, ROWS), :]
            if it == 0:
                s = s * scale
                s_ref[pl.ds(r, ROWS), :] = s
            row = s + terms
            high = jnp.max(row, axis=1, keepdims=True)
            lse = high + jnp.log(jnp.sum(jnp.exp(row - high), axis=1, keepdims=True))
            place_in = lax.broadcasted_iota(jnp.int32, (ROWS, 1), 0) + r
            real = place_in.astype(jnp.float32) < own_students
            column = s - lse + jnp.where(real, 0.0, NEG)
            c_ref[pl.ds(r, ROWS), :] = column
            top = jnp.maximum(top, jnp.max(column.reshape(ROWS // 8, 8, m), axis=0))
            if it == ITERS - 1:
                lse_ref[pl.ds(r, ROWS), :] = jnp.broadcast_to(lse, (ROWS, 128))
        top = jnp.max(top, axis=0, keepdims=True)
        total = jnp.zeros((8, m), jnp.float32)
        for r in range(0, rows, ROWS):
            grown = jnp.exp(c_ref[pl.ds(r, ROWS), :] - top)
            total += jnp.sum(grown.reshape(ROWS // 8, 8, m), axis=0)
        partial = top + jnp.log(jnp.sum(total, axis=0, keepdims=True))
        for p, axes in enumerate(phases):
            box = stats[p].at[it]
            box[place(axes)] = partial
            send_all(box, stat_send.at[p, it], stat_recv.at[p, it], axes)
            if it == ITERS - 1 and p == 0:
                potential_ref[...] = (-EPS) * jnp.transpose(lse_ref[...])[0:1, :]
            arrived(box, stat_recv.at[p, it], axes)
            partial = log_sum(box[...])
        terms = (log_count - partial) + log_teacher

    weights = jnp.exp(c_ref[...] + terms).astype(jnp.bfloat16)
    span = width // 4
    if fs % 128:
        for c in range(nt):
            o_ref[:, c * fs : (c + 1) * fs] = jnp.dot(
                weights, all_t[c], preferred_element_type=jnp.float32
            ).astype(jnp.bfloat16)
        store = pltpu.make_async_copy(o_ref, targets_hbm, out_sem.at[0])
        store.start()
        stores = [store]
    else:
        stores = []
        for c in range(nt):
            part = pl.ds(c * fs, fs)
            o_ref[:, part] = jnp.dot(weights, all_t[c], preferred_element_type=jnp.float32).astype(jnp.bfloat16)
            store = pltpu.make_async_copy(o_ref.at[:, part], targets_hbm.at[:, part], out_sem.at[c])
            store.start()
            stores.append(store)

    wait_bytes(all_t.at[pl.ds(0, nt - 1), pl.ds(0, tb), :], tok_send)
    wait_bytes(all_t.at[:, pl.ds(0, (nb - 1) * tb), :], blk_send)
    for p, axes in enumerate(phases):
        arrived(meta[p], meta_send.at[p], axes)
        for it in range(ITERS):
            arrived(stats[p].at[it], stat_send.at[p, it], axes)
    for store in stores:
        store.wait()


def shards(nt, nb, student, teacher, student_mask, teacher_mask):
    rows, width = student.shape
    tb, fs = teacher.shape
    m = nb * tb
    phases = [("tok", "blk")] if nt * nb <= DIRECT else [("blk",), ("tok",)]
    sizes = [math.prod({"tok": nt, "blk": nb}[a] for a in axes) for axes in phases]
    vmem = pl.BlockSpec(memory_space=pltpu.VMEM)
    hbm = pl.BlockSpec(memory_space=pl.ANY)
    dma = pltpu.SemaphoreType.DMA
    targets, potential = pl.pallas_call(
        functools.partial(kernel, nt, nb, phases, 1.0 / (math.sqrt(width) * EPS)),
        out_shape=(
            jax.ShapeDtypeStruct((rows, width), jnp.bfloat16),
            jax.ShapeDtypeStruct((1, rows), jnp.float32),
        ),
        in_specs=[hbm, hbm, vmem, vmem],
        out_specs=(hbm, vmem),
        scratch_shapes=[
            pltpu.VMEM((rows, width), jnp.bfloat16),
            pltpu.VMEM((nt, m, fs), jnp.bfloat16),
            pltpu.VMEM((rows, m), jnp.float32),
            pltpu.VMEM((rows, m), jnp.float32),
            pltpu.VMEM((rows, 128), jnp.float32),
            pltpu.VMEM((rows, width), jnp.bfloat16),
            [pltpu.VMEM((size, 1, 256), jnp.float32) for size in sizes],
            [pltpu.VMEM((ITERS, size, 1, m), jnp.float32) for size in sizes],
            dma((2,)),
            dma((nt,)),
            dma(()),
            dma((nt,)),
            dma(()),
            dma((nt, nb)),
            dma((2,)),
            dma((2,)),
            dma((2, ITERS)),
            dma((2, ITERS)),
        ],
        compiler_params=pltpu.CompilerParams(
            collective_id=0, has_side_effects=True, vmem_limit_bytes=32 * 2**20
        ),
        cost_estimate=pl.CostEstimate(
            flops=4 * rows * m * width, bytes_accessed=4 * rows * width + 2 * m * width, transcendentals=7 * rows * m
        ),
    )(student, teacher, student_mask.reshape(1, rows), teacher_mask.reshape(1, tb))
    return targets, potential.reshape(rows)


def solution(mesh):
    in_specs = (
        P(("grp", "tok", "blk"), None),
        P(("grp", "blk"), "tok"),
        P(("grp", "tok", "blk")),
        P(("grp", "blk")),
    )
    out_specs = (P(("grp", "tok", "blk"), None), P(("grp", "tok", "blk")))
    body = functools.partial(shards, mesh.shape["tok"], mesh.shape["blk"])
    return jax.shard_map(body, mesh=mesh, in_specs=in_specs, out_specs=out_specs, check_vma=False)
```

```python
import functools
import math

import jax
import jax.numpy as jnp
from jax import lax
from jax.experimental import pallas as pl
from jax.experimental.pallas import tpu as pltpu
from jax.sharding import PartitionSpec as P

ITERS = 3
EPS = 0.25
NEG = -1e30
ROWS = 64
DIRECT = 16


def kernel(
    nt, nb, phases, scale,
    student_hbm, teacher_hbm, student_mask_hbm, teacher_mask_hbm,
    column_hbm, copied_t, terms_ref, potential_ref,
    student_mask, teacher_mask, x_ref, all_t, s_ref, c_ref, lse_ref, meta, stats,
    local_sem, out_sem, tok_send, tok_recv, blk_send, blk_recv, meta_send, meta_recv, stat_send, stat_recv,
):
    rows, width = x_ref.shape
    tb, fs = teacher_hbm.shape
    m = nb * tb
    t, b = lax.axis_index("tok"), lax.axis_index("blk")
    bits = [1 << k for k in reversed(range(nb.bit_length() - 1))]

    load_x = pltpu.make_async_copy(student_hbm, x_ref, local_sem.at[0])
    load_masks = [
        pltpu.make_async_copy(student_mask_hbm, student_mask, local_sem.at[2]),
        pltpu.make_async_copy(teacher_mask_hbm, teacher_mask, local_sem.at[3]),
    ]
    for load in load_masks:
        load.start()
    load_x.start()

    def block(c, owner):
        return all_t.at[c, pl.ds(pl.multiple_of(owner * tb, tb), tb), :]

    load_t = pltpu.make_async_copy(teacher_hbm, block(t, b), local_sem.at[1])
    load_t.start()

    def others(axes):
        spans = [range(nt) if "tok" in axes else range(1), range(nb) if "blk" in axes else range(1)]
        return [(i, j) for i in spans[0] for j in spans[1] if i or j]

    def peer(i, j):
        return {"tok": t ^ i, "blk": b ^ j}

    greeted = sorted({p for axes in phases for p in others(axes)} | {p for p in others(("tok",))} | {p for p in others(("blk",))})
    barrier = pltpu.get_barrier_semaphore()
    for i, j in greeted:
        pl.semaphore_signal(barrier, inc=1, device_id=peer(i, j), device_id_type=pl.DeviceIdType.MESH)
    pl.semaphore_wait(barrier, len(greeted))

    def place(axes):
        if len(axes) == 2:
            return t * nb + b
        return t if "tok" in axes else b

    def send_all(ref, send, recv, axes):
        mine = place(axes)
        for i, j in others(axes):
            pltpu.make_async_remote_copy(
                src_ref=ref.at[mine], dst_ref=ref.at[mine], send_sem=send, recv_sem=recv,
                device_id=peer(i, j), device_id_type=pl.DeviceIdType.MESH,
            ).start()

    def wait_bytes(ref, sem):
        pltpu.make_async_copy(ref, ref, sem).wait()

    def arrived(ref, recv, axes):
        wait_bytes(ref.at[pl.ds(0, len(others(axes)))], recv)

    def meta_values():
        ns = jnp.sum(student_mask[...].astype(jnp.float32), axis=1, keepdims=True)
        nteach = jnp.sum(teacher_mask[...].astype(jnp.float32), axis=1, keepdims=True)
        return ns, nteach


    def tok_copy(i, source):
        return pltpu.make_async_remote_copy(
            src_ref=teacher_hbm, dst_ref=block(source, b), send_sem=tok_send, recv_sem=tok_recv.at[source],
            device_id=peer(i, 0), device_id_type=pl.DeviceIdType.MESH,
        )

    def blk_copy(c, owner, bit):
        return pltpu.make_async_remote_copy(
            src_ref=block(c, owner), dst_ref=block(c, owner), send_sem=blk_send, recv_sem=blk_recv.at[c, owner],
            device_id=peer(0, bit), device_id_type=pl.DeviceIdType.MESH,
        )

    for i in range(1, nt):
        tok_copy(i, t).start()

    def hold_own(d):
        c = t ^ d
        if isinstance(d, int) and d == 0:
            load_t.wait()
        else:
            tok_copy(0, c).wait_recv()
        for bit in bits:
            blk_copy(c, b, bit).start()

    def forward(d, lowest):
        c = t ^ d
        for h in range(1, nb):
            if (h & -h) != lowest:
                continue
            blk_copy(c, b ^ h, lowest).wait_recv()
            for bit in bits:
                if bit < lowest:
                    blk_copy(c, b ^ h, bit).start()

    hold_own(0)

    for load in load_masks:
        load.wait()
    own_students, own_teachers = meta_values()
    meta[0][place(phases[0])] = jnp.concatenate(
        [jnp.broadcast_to(own_students, (1, 128)), jnp.broadcast_to(own_teachers, (1, 128))], axis=1
    )
    send_all(meta[0], meta_send.at[0], meta_recv.at[0], phases[0])

    def multiply(c, columns, first):
        part = lax.dot_general(
            x_ref[:, columns], all_t[c], (((1,), (1,)), ((), ())), preferred_element_type=jnp.float32
        )
        if first:
            s_ref[...] = part
        else:
            s_ref[...] += part

    aligned = fs % 128 == 0 and nt <= 8
    if aligned:
        for d in range(nt + len(bits)):
            if 0 < d < nt:
                hold_own(d)
            for k, bit in enumerate(bits):
                if 0 <= d - k - 1 < nt:
                    forward(d - k - 1, bit)
            done = d - len(bits)
            if 0 <= done < nt:
                if done == 0:
                    load_x.wait()
                c = t ^ done
                multiply(c, pl.ds(pl.multiple_of(c * fs, 128), fs), done == 0)
    else:
        def step(d, carry):
            hold_own(d)
            return carry

        lax.fori_loop(1, nt, step, 0)
        for bit in bits:
            def pass_on(d, carry, bit=bit):
                forward(d, bit)
                return carry

            lax.fori_loop(0, nt, pass_on, 0)
        load_x.wait()
        for c in range(nt):
            multiply(c, pl.ds(c * fs, fs), c == 0)

    store_t = pltpu.make_async_copy(all_t, copied_t, out_sem.at[0])
    store_t.start()

    arrived(meta[0], meta_recv.at[0], phases[0])
    lane = lax.broadcasted_iota(jnp.int32, (1, m), 1)
    limit = jnp.zeros((1, m), jnp.float32)
    teacher_total = jnp.zeros((1, 1), jnp.float32)
    for j in range(nb):
        slot = t * nb + j if len(phases[0]) == 2 else j
        held = meta[0][slot][:, 128:129]
        teacher_total += held
        limit = jnp.where(lane // tb == j, held, limit)
    valid_teacher = (lane % tb).astype(jnp.float32) < limit
    log_teacher = jnp.where(valid_teacher, -jnp.log(teacher_total), NEG)
    student_total = jnp.sum(meta[0][...][:, :, 0:1], axis=0)
    if len(phases) == 2:
        meta[1][place(phases[1])] = jnp.broadcast_to(student_total, (1, 256))
        send_all(meta[1], meta_send.at[1], meta_recv.at[1], phases[1])
        arrived(meta[1], meta_recv.at[1], phases[1])
        student_total = jnp.sum(meta[1][...][:, :, 0:1], axis=0)
    log_count = jnp.log(student_total)

    def log_sum(values):
        top = jnp.max(values, axis=0)
        return top + jnp.log(jnp.sum(jnp.exp(values - top[None]), axis=0))

    terms = log_teacher
    for it in range(ITERS):
        top = jnp.full((8, m), -jnp.inf, jnp.float32)
        for r in range(0, rows, ROWS):
            s = s_ref[pl.ds(r, ROWS), :]
            if it == 0:
                s = s * scale
                s_ref[pl.ds(r, ROWS), :] = s
            row = s + terms
            high = jnp.max(row, axis=1, keepdims=True)
            lse = high + jnp.log(jnp.sum(jnp.exp(row - high), axis=1, keepdims=True))
            place_in = lax.broadcasted_iota(jnp.int32, (ROWS, 1), 0) + r
            real = place_in.astype(jnp.float32) < own_students
            column = s - lse + jnp.where(real, 0.0, NEG)
            c_ref[pl.ds(r, ROWS), :] = column
            top = jnp.maximum(top, jnp.max(column.reshape(ROWS // 8, 8, m), axis=0))
            if it == ITERS - 1:
                lse_ref[pl.ds(r, ROWS), :] = jnp.broadcast_to(lse, (ROWS, 128))
        top = jnp.max(top, axis=0, keepdims=True)
        total = jnp.zeros((8, m), jnp.float32)
        for r in range(0, rows, ROWS):
            grown = jnp.exp(c_ref[pl.ds(r, ROWS), :] - top)
            total += jnp.sum(grown.reshape(ROWS // 8, 8, m), axis=0)
        partial = top + jnp.log(jnp.sum(total, axis=0, keepdims=True))
        for p, axes in enumerate(phases):
            box = stats[p].at[it]
            box[place(axes)] = partial
            send_all(box, stat_send.at[p, it], stat_recv.at[p, it], axes)
            if it == ITERS - 1 and p == 0:
                store_c = pltpu.make_async_copy(c_ref, column_hbm, out_sem.at[1])
                store_c.start()
                potential_ref[...] = (-EPS) * jnp.transpose(lse_ref[...])[0:1, :]
            arrived(box, stat_recv.at[p, it], axes)
            partial = log_sum(box[...])
        terms = (log_count - partial) + log_teacher

    terms_ref[...] = terms
    wait_bytes(all_t.at[pl.ds(0, nt - 1), pl.ds(0, tb), :], tok_send)
    wait_bytes(all_t.at[:, pl.ds(0, (nb - 1) * tb), :], blk_send)
    for p, axes in enumerate(phases):
        arrived(meta[p], meta_send.at[p], axes)
        for it in range(ITERS):
            arrived(stats[p].at[it], stat_send.at[p, it], axes)
    store_t.wait()
    store_c.wait()


def average(
    nt, column_hbm, all_t_hbm, terms_hbm, potential_hbm, targets_hbm, potential_out,
    c_ref, t_ref, terms_ref, o_ref, in_sem, t_sem, out_sem,
):
    fs = t_ref.shape[2]
    loads = [
        pltpu.make_async_copy(terms_hbm, terms_ref, in_sem.at[0]),
        pltpu.make_async_copy(column_hbm, c_ref, in_sem.at[1]),
    ]
    blocks = [pltpu.make_async_copy(all_t_hbm.at[c], t_ref.at[c], t_sem.at[c]) for c in range(nt)]
    pass_on = pltpu.make_async_copy(potential_hbm, potential_out, in_sem.at[2])
    for load in loads + blocks + [pass_on]:
        load.start()
    for load in loads:
        load.wait()
    weights = jnp.exp(c_ref[...] + terms_ref[...]).astype(jnp.bfloat16)
    stores = []
    for c in range(nt):
        blocks[c].wait()
        part = pl.ds(c * fs, fs)
        o_ref[:, part] = jnp.dot(weights, t_ref[c], preferred_element_type=jnp.float32).astype(jnp.bfloat16)
        if fs % 128 == 0:
            stores.append(pltpu.make_async_copy(o_ref.at[:, part], targets_hbm.at[:, part], out_sem.at[c]))
            stores[-1].start()
    if not stores:
        stores.append(pltpu.make_async_copy(o_ref, targets_hbm, out_sem.at[0]))
        stores[-1].start()
    for store in stores + [pass_on]:
        store.wait()


def shards(nt, nb, student, teacher, student_mask, teacher_mask):
    rows, width = student.shape
    tb, fs = teacher.shape
    m = nb * tb
    phases = [("tok", "blk")] if nt * nb <= DIRECT else [("blk",), ("tok",)]
    sizes = [math.prod({"tok": nt, "blk": nb}[a] for a in axes) for axes in phases]
    vmem = pl.BlockSpec(memory_space=pltpu.VMEM)
    hbm = pl.BlockSpec(memory_space=pltpu.HBM)
    dma = pltpu.SemaphoreType.DMA
    column, whole_t, terms, potential = pl.pallas_call(
        functools.partial(kernel, nt, nb, phases, 1.0 / (math.sqrt(width) * EPS)),
        out_shape=(
            jax.ShapeDtypeStruct((rows, m), jnp.float32),
            jax.ShapeDtypeStruct((nt, m, fs), jnp.bfloat16),
            jax.ShapeDtypeStruct((1, m), jnp.float32),
            jax.ShapeDtypeStruct((1, rows), jnp.float32),
        ),
        in_specs=[hbm] * 4,
        out_specs=(hbm, hbm, vmem, vmem),
        scratch_shapes=[
            pltpu.VMEM((1, rows), jnp.int32),
            pltpu.VMEM((1, tb), jnp.int32),
            pltpu.VMEM((rows, width), jnp.bfloat16),
            pltpu.VMEM((nt, m, fs), jnp.bfloat16),
            pltpu.VMEM((rows, m), jnp.float32),
            pltpu.VMEM((rows, m), jnp.float32),
            pltpu.VMEM((rows, 128), jnp.float32),
            [pltpu.VMEM((size, 1, 256), jnp.float32) for size in sizes],
            [pltpu.VMEM((ITERS, size, 1, m), jnp.float32) for size in sizes],
            dma((4,)),
            dma((2,)),
            dma(()),
            dma((nt,)),
            dma(()),
            dma((nt, nb)),
            dma((2,)),
            dma((2,)),
            dma((2, ITERS)),
            dma((2, ITERS)),
        ],
        compiler_params=pltpu.CompilerParams(
            collective_id=0, has_side_effects=True, vmem_limit_bytes=60 * 2**20
        ),
        cost_estimate=pl.CostEstimate(
            flops=4 * rows * m * width, bytes_accessed=4 * rows * width + 2 * m * width, transcendentals=7 * rows * m
        ),
    )(student, teacher, student_mask.reshape(1, rows), teacher_mask.reshape(1, tb))
    targets, potential = pl.pallas_call(
        functools.partial(average, nt),
        out_shape=(
            jax.ShapeDtypeStruct((rows, width), jnp.bfloat16),
            jax.ShapeDtypeStruct((1, rows), jnp.float32),
        ),
        in_specs=[hbm] * 4,
        out_specs=(hbm, hbm),
        scratch_shapes=[
            pltpu.VMEM((rows, m), jnp.float32),
            pltpu.VMEM((nt, m, fs), jnp.bfloat16),
            pltpu.VMEM((1, m), jnp.float32),
            pltpu.VMEM((rows, width), jnp.bfloat16),
            dma((3,)),
            dma((nt,)),
            dma((nt,)),
        ],
        compiler_params=pltpu.CompilerParams(vmem_limit_bytes=60 * 2**20),
    )(column, whole_t, terms, potential)
    return targets, potential.reshape(rows)


def solution(mesh):
    in_specs = (
        P(("grp", "tok", "blk"), None),
        P(("grp", "blk"), "tok"),
        P(("grp", "tok", "blk")),
        P(("grp", "blk")),
    )
    out_specs = (P(("grp", "tok", "blk"), None), P(("grp", "tok", "blk")))
    body = functools.partial(shards, mesh.shape["tok"], mesh.shape["blk"])
    return jax.shard_map(body, mesh=mesh, in_specs=in_specs, out_specs=out_specs, check_vma=False)
```

```python
import functools
import math

import jax
import jax.numpy as jnp
from jax import lax
from jax.experimental import pallas as pl
from jax.experimental.pallas import tpu as pltpu
from jax.sharding import PartitionSpec as P

ITERS = 3
EPS = 0.25
NEG = -1e30
ROWS = 64
DIRECT = 16


def kernel(
    nt, nb, phases, scale,
    student_hbm, teacher_hbm, student_mask_hbm, teacher_mask_hbm,
    column_hbm, copied_t, terms_ref, potential_ref,
    student_mask, teacher_mask, x_ref, all_t, s_ref, c_ref, lse_ref, meta, stats,
    local_sem, out_sem, tok_send, tok_recv, blk_send, blk_recv, meta_send, meta_recv, stat_send, stat_recv,
):
    rows, width = x_ref.shape
    tb, fs = teacher_hbm.shape
    m = nb * tb
    t, b = lax.axis_index("tok"), lax.axis_index("blk")
    bits = [1 << k for k in reversed(range(nb.bit_length() - 1))]

    def block(c, owner):
        return all_t.at[c, pl.ds(pl.multiple_of(owner * tb, tb), tb), :]

    def others(axes):
        spans = [range(nt) if "tok" in axes else range(1), range(nb) if "blk" in axes else range(1)]
        return [(i, j) for i in reversed(spans[0]) for j in reversed(spans[1]) if i or j]

    def peer(i, j):
        return {"tok": t ^ i, "blk": b ^ j}

    greeted = sorted({p for axes in phases for p in others(axes)} | {p for p in others(("tok",))} | {p for p in others(("blk",))})
    barrier = pltpu.get_barrier_semaphore()
    for i, j in greeted:
        pl.semaphore_signal(barrier, inc=1, device_id=peer(i, j), device_id_type=pl.DeviceIdType.MESH)
    load_t = pltpu.make_async_copy(teacher_hbm, block(t, b), local_sem.at[1])
    load_t.start()
    load_x = pltpu.make_async_copy(student_hbm, x_ref, local_sem.at[0])
    load_masks = [
        pltpu.make_async_copy(student_mask_hbm, student_mask, local_sem.at[2]),
        pltpu.make_async_copy(teacher_mask_hbm, teacher_mask, local_sem.at[3]),
    ]
    for load in load_masks:
        load.start()
    load_x.start()
    pl.semaphore_wait(barrier, len(greeted))

    def place(axes):
        if len(axes) == 2:
            return t * nb + b
        return t if "tok" in axes else b

    def send_all(ref, send, recv, axes):
        mine = place(axes)
        for i, j in others(axes):
            pltpu.make_async_remote_copy(
                src_ref=ref.at[mine], dst_ref=ref.at[mine], send_sem=send, recv_sem=recv,
                device_id=peer(i, j), device_id_type=pl.DeviceIdType.MESH,
            ).start()

    def wait_bytes(ref, sem):
        pltpu.make_async_copy(ref, ref, sem).wait()

    def arrived(ref, recv, axes):
        wait_bytes(ref.at[pl.ds(0, len(others(axes)))], recv)

    def meta_values():
        ns = jnp.sum(student_mask[...].astype(jnp.float32), axis=1, keepdims=True)
        nteach = jnp.sum(teacher_mask[...].astype(jnp.float32), axis=1, keepdims=True)
        return ns, nteach


    def tok_copy(i, source):
        return pltpu.make_async_remote_copy(
            src_ref=teacher_hbm, dst_ref=block(source, b), send_sem=tok_send, recv_sem=tok_recv.at[source],
            device_id=peer(i, 0), device_id_type=pl.DeviceIdType.MESH,
        )

    def blk_copy(c, owner, bit, own=False):
        return pltpu.make_async_remote_copy(
            src_ref=teacher_hbm if own else block(c, owner), dst_ref=block(c, owner), send_sem=blk_send, recv_sem=blk_recv.at[c, owner],
            device_id=peer(0, bit), device_id_type=pl.DeviceIdType.MESH,
        )

    for bit in bits[:1]:
        blk_copy(t, b, bit, True).start()
    for i in range(1, nt):
        tok_copy(i, t).start()
    for bit in bits[1:]:
        blk_copy(t, b, bit, True).start()

    def hold_own(d):
        c = t ^ d
        tok_copy(0, c).wait_recv()
        for bit in bits:
            blk_copy(c, b, bit).start()

    def forward(d, lowest):
        c = t ^ d
        for h in range(1, nb):
            if (h & -h) != lowest:
                continue
            blk_copy(c, b ^ h, lowest).wait_recv()
            for bit in bits:
                if bit < lowest:
                    blk_copy(c, b ^ h, bit).start()

    for load in load_masks:
        load.wait()
    own_students, own_teachers = meta_values()
    meta[0][place(phases[0])] = jnp.concatenate(
        [jnp.broadcast_to(own_students, (1, 128)), jnp.broadcast_to(own_teachers, (1, 128))], axis=1
    )
    send_all(meta[0], meta_send.at[0], meta_recv.at[0], phases[0])

    def multiply(c, columns, first):
        part = lax.dot_general(
            x_ref[:, columns], all_t[c], (((1,), (1,)), ((), ())), preferred_element_type=jnp.float32
        )
        if first:
            s_ref[...] = part
        else:
            s_ref[...] += part

    aligned = fs % 128 == 0 and nt <= 8
    if aligned:
        for d in range(nt + len(bits)):
            if 0 < d < nt:
                hold_own(d)
            for k, bit in enumerate(bits):
                if 0 <= d - k - 1 < nt:
                    forward(d - k - 1, bit)
            done = d - len(bits)
            if 0 <= done < nt:
                if done == 0:
                    load_t.wait()
                    load_x.wait()
                c = t ^ done
                multiply(c, pl.ds(pl.multiple_of(c * fs, 128), fs), done == 0)
    else:
        def step(d, carry):
            hold_own(d)
            return carry

        lax.fori_loop(1, nt, step, 0)
        for bit in bits:
            def pass_on(d, carry, bit=bit):
                forward(d, bit)
                return carry

            lax.fori_loop(0, nt, pass_on, 0)
        load_t.wait()
        load_x.wait()
        for c in range(nt):
            multiply(c, pl.ds(c * fs, fs), c == 0)

    store_t = pltpu.make_async_copy(all_t, copied_t, out_sem.at[0])
    store_t.start()

    arrived(meta[0], meta_recv.at[0], phases[0])
    lane = lax.broadcasted_iota(jnp.int32, (1, m), 1)
    limit = jnp.zeros((1, m), jnp.float32)
    teacher_total = jnp.zeros((1, 1), jnp.float32)
    for j in range(nb):
        slot = t * nb + j if len(phases[0]) == 2 else j
        held = meta[0][slot][:, 128:129]
        teacher_total += held
        limit = jnp.where(lane // tb == j, held, limit)
    valid_teacher = (lane % tb).astype(jnp.float32) < limit
    log_teacher = jnp.where(valid_teacher, -jnp.log(teacher_total), NEG)
    student_total = jnp.sum(meta[0][...][:, :, 0:1], axis=0)
    if len(phases) == 2:
        meta[1][place(phases[1])] = jnp.broadcast_to(student_total, (1, 256))
        send_all(meta[1], meta_send.at[1], meta_recv.at[1], phases[1])
        arrived(meta[1], meta_recv.at[1], phases[1])
        student_total = jnp.sum(meta[1][...][:, :, 0:1], axis=0)
    log_count = jnp.log(student_total)

    def log_sum(values):
        top = jnp.max(values, axis=0)
        return top + jnp.log(jnp.sum(jnp.exp(values - top[None]), axis=0))

    terms = log_teacher
    for it in range(ITERS):
        top = jnp.full((8, m), -jnp.inf, jnp.float32)
        for r in range(0, rows, ROWS):
            s = s_ref[pl.ds(r, ROWS), :]
            if it == 0:
                s = s * scale
                s_ref[pl.ds(r, ROWS), :] = s
            row = s + terms
            high = jnp.max(row, axis=1, keepdims=True)
            lse = high + jnp.log(jnp.sum(jnp.exp(row - high), axis=1, keepdims=True))
            place_in = lax.broadcasted_iota(jnp.int32, (ROWS, 1), 0) + r
            real = place_in.astype(jnp.float32) < own_students
            column = s - lse + jnp.where(real, 0.0, NEG)
            c_ref[pl.ds(r, ROWS), :] = column
            top = jnp.maximum(top, jnp.max(column.reshape(ROWS // 8, 8, m), axis=0))
            if it == ITERS - 1:
                lse_ref[pl.ds(r, ROWS), :] = jnp.broadcast_to(lse, (ROWS, 128))
        top = jnp.max(top, axis=0, keepdims=True)
        total = jnp.zeros((8, m), jnp.float32)
        for r in range(0, rows, ROWS):
            grown = jnp.exp(c_ref[pl.ds(r, ROWS), :] - top)
            total += jnp.sum(grown.reshape(ROWS // 8, 8, m), axis=0)
        partial = top + jnp.log(jnp.sum(total, axis=0, keepdims=True))
        for p, axes in enumerate(phases):
            box = stats[p].at[it]
            box[place(axes)] = partial
            send_all(box, stat_send.at[p, it], stat_recv.at[p, it], axes)
            if it == ITERS - 1 and p == 0:
                store_c = pltpu.make_async_copy(c_ref, column_hbm, out_sem.at[1])
                store_c.start()
                potential_ref[...] = (-EPS) * jnp.transpose(lse_ref[...])[0:1, :]
            arrived(box, stat_recv.at[p, it], axes)
            partial = log_sum(box[...])
        terms = (log_count - partial) + log_teacher

    terms_ref[...] = terms
    wait_bytes(all_t.at[pl.ds(0, nt - 1), pl.ds(0, tb), :], tok_send)
    wait_bytes(all_t.at[:, pl.ds(0, (nb - 1) * tb), :], blk_send)
    for p, axes in enumerate(phases):
        arrived(meta[p], meta_send.at[p], axes)
        for it in range(ITERS):
            arrived(stats[p].at[it], stat_send.at[p, it], axes)
    store_t.wait()
    store_c.wait()


def average(
    nt, column_hbm, all_t_hbm, terms_hbm, potential_hbm, targets_hbm, potential_out,
    c_ref, t_ref, terms_ref, o_ref, in_sem, t_sem, out_sem,
):
    fs = t_ref.shape[2]
    loads = [
        pltpu.make_async_copy(terms_hbm, terms_ref, in_sem.at[0]),
        pltpu.make_async_copy(column_hbm, c_ref, in_sem.at[1]),
    ]
    blocks = [pltpu.make_async_copy(all_t_hbm.at[c], t_ref.at[c], t_sem.at[c]) for c in range(nt)]
    pass_on = pltpu.make_async_copy(potential_hbm, potential_out, in_sem.at[2])
    for load in loads + blocks + [pass_on]:
        load.start()
    for load in loads:
        load.wait()
    weights = jnp.exp(c_ref[...] + terms_ref[...]).astype(jnp.bfloat16)
    stores = []
    for c in range(nt):
        blocks[c].wait()
        part = pl.ds(c * fs, fs)
        o_ref[:, part] = jnp.dot(weights, t_ref[c], preferred_element_type=jnp.float32).astype(jnp.bfloat16)
        if fs % 128 == 0:
            stores.append(pltpu.make_async_copy(o_ref.at[:, part], targets_hbm.at[:, part], out_sem.at[c]))
            stores[-1].start()
    if not stores:
        stores.append(pltpu.make_async_copy(o_ref, targets_hbm, out_sem.at[0]))
        stores[-1].start()
    for store in stores + [pass_on]:
        store.wait()


def shards(nt, nb, student, teacher, student_mask, teacher_mask):
    rows, width = student.shape
    tb, fs = teacher.shape
    m = nb * tb
    phases = [("tok", "blk")] if nt * nb <= DIRECT else [("blk",), ("tok",)]
    sizes = [math.prod({"tok": nt, "blk": nb}[a] for a in axes) for axes in phases]
    vmem = pl.BlockSpec(memory_space=pltpu.VMEM)
    hbm = pl.BlockSpec(memory_space=pltpu.HBM)
    dma = pltpu.SemaphoreType.DMA
    column, whole_t, terms, potential = pl.pallas_call(
        functools.partial(kernel, nt, nb, phases, 1.0 / (math.sqrt(width) * EPS)),
        out_shape=(
            jax.ShapeDtypeStruct((rows, m), jnp.float32),
            jax.ShapeDtypeStruct((nt, m, fs), jnp.bfloat16),
            jax.ShapeDtypeStruct((1, m), jnp.float32),
            jax.ShapeDtypeStruct((1, rows), jnp.float32),
        ),
        in_specs=[hbm] * 4,
        out_specs=(hbm, hbm, vmem, vmem),
        scratch_shapes=[
            pltpu.VMEM((1, rows), jnp.int32),
            pltpu.VMEM((1, tb), jnp.int32),
            pltpu.VMEM((rows, width), jnp.bfloat16),
            pltpu.VMEM((nt, m, fs), jnp.bfloat16),
            pltpu.VMEM((rows, m), jnp.float32),
            pltpu.VMEM((rows, m), jnp.float32),
            pltpu.VMEM((rows, 128), jnp.float32),
            [pltpu.VMEM((size, 1, 256), jnp.float32) for size in sizes],
            [pltpu.VMEM((ITERS, size, 1, m), jnp.float32) for size in sizes],
            dma((4,)),
            dma((2,)),
            dma(()),
            dma((nt,)),
            dma(()),
            dma((nt, nb)),
            dma((2,)),
            dma((2,)),
            dma((2, ITERS)),
            dma((2, ITERS)),
        ],
        compiler_params=pltpu.CompilerParams(
            collective_id=0, has_side_effects=True, vmem_limit_bytes=60 * 2**20
        ),
        cost_estimate=pl.CostEstimate(
            flops=4 * rows * m * width, bytes_accessed=4 * rows * width + 2 * m * width, transcendentals=7 * rows * m
        ),
    )(student, teacher, student_mask.reshape(1, rows), teacher_mask.reshape(1, tb))
    targets, potential = pl.pallas_call(
        functools.partial(average, nt),
        out_shape=(
            jax.ShapeDtypeStruct((rows, width), jnp.bfloat16),
            jax.ShapeDtypeStruct((1, rows), jnp.float32),
        ),
        in_specs=[hbm] * 4,
        out_specs=(hbm, hbm),
        scratch_shapes=[
            pltpu.VMEM((rows, m), jnp.float32),
            pltpu.VMEM((nt, m, fs), jnp.bfloat16),
            pltpu.VMEM((1, m), jnp.float32),
            pltpu.VMEM((rows, width), jnp.bfloat16),
            dma((3,)),
            dma((nt,)),
            dma((nt,)),
        ],
        compiler_params=pltpu.CompilerParams(vmem_limit_bytes=60 * 2**20),
    )(column, whole_t, terms, potential)
    return targets, potential.reshape(rows)


def solution(mesh):
    in_specs = (
        P(("grp", "tok", "blk"), None),
        P(("grp", "blk"), "tok"),
        P(("grp", "tok", "blk")),
        P(("grp", "blk")),
    )
    out_specs = (P(("grp", "tok", "blk"), None), P(("grp", "tok", "blk")))
    body = functools.partial(shards, mesh.shape["tok"], mesh.shape["blk"])
    return jax.shard_map(body, mesh=mesh, in_specs=in_specs, out_specs=out_specs, check_vma=False)
```

```python
import functools
import math

import jax
import jax.numpy as jnp
from jax import lax
from jax.experimental import pallas as pl
from jax.experimental.pallas import tpu as pltpu
from jax.sharding import PartitionSpec as P

ITERS = 3
EPS = 0.25
NEG = -1e30
ROWS = 64
DIRECT = 16


def kernel(
    nt, nb, phases, scale,
    student_hbm, teacher_hbm, student_mask_hbm, teacher_mask_hbm,
    column_hbm, copied_t, terms_ref, potential_ref,
    student_mask, teacher_mask, x_ref, all_t, s_ref, c_ref, lse_ref, meta, stats,
    local_sem, out_sem, tok_send, tok_recv, blk_send, blk_recv, meta_send, meta_recv, stat_send, stat_recv,
):
    rows, width = x_ref.shape
    tb, fs = teacher_hbm.shape
    m = nb * tb
    t, b = lax.axis_index("tok"), lax.axis_index("blk")
    bits = [1 << k for k in reversed(range(nb.bit_length() - 1))]

    def block(c, owner):
        return all_t.at[c, pl.ds(pl.multiple_of(owner * tb, tb), tb), :]

    def others(axes):
        spans = [range(nt) if "tok" in axes else range(1), range(nb) if "blk" in axes else range(1)]
        return [(i, j) for i in reversed(spans[0]) for j in reversed(spans[1]) if i or j]

    def peer(i, j):
        return {"tok": t ^ i, "blk": b ^ j}

    greeted = sorted({p for axes in phases for p in others(axes)} | {p for p in others(("tok",))} | {p for p in others(("blk",))})
    barrier = pltpu.get_barrier_semaphore()
    for i, j in greeted:
        pl.semaphore_signal(barrier, inc=1, device_id=peer(i, j), device_id_type=pl.DeviceIdType.MESH)
    load_t = pltpu.make_async_copy(teacher_hbm, block(t, b), local_sem.at[1])
    load_t.start()
    load_x = pltpu.make_async_copy(student_hbm, x_ref, local_sem.at[0])
    load_masks = [
        pltpu.make_async_copy(student_mask_hbm, student_mask, local_sem.at[2]),
        pltpu.make_async_copy(teacher_mask_hbm, teacher_mask, local_sem.at[3]),
    ]
    for load in load_masks:
        load.start()
    load_x.start()
    pl.semaphore_wait(barrier, len(greeted))

    def place(axes):
        if len(axes) == 2:
            return t * nb + b
        return t if "tok" in axes else b

    def send_all(ref, send, recv, axes):
        mine = place(axes)
        for i, j in others(axes):
            pltpu.make_async_remote_copy(
                src_ref=ref.at[mine], dst_ref=ref.at[mine], send_sem=send, recv_sem=recv,
                device_id=peer(i, j), device_id_type=pl.DeviceIdType.MESH,
            ).start()

    def wait_bytes(ref, sem):
        pltpu.make_async_copy(ref, ref, sem).wait()

    def arrived(ref, recv, axes):
        wait_bytes(ref.at[pl.ds(0, len(others(axes)))], recv)

    def meta_values():
        ns = jnp.sum(student_mask[...].astype(jnp.float32), axis=1, keepdims=True)
        nteach = jnp.sum(teacher_mask[...].astype(jnp.float32), axis=1, keepdims=True)
        return ns, nteach


    def tok_copy(i, source):
        return pltpu.make_async_remote_copy(
            src_ref=teacher_hbm, dst_ref=block(source, b), send_sem=tok_send, recv_sem=tok_recv.at[source],
            device_id=peer(i, 0), device_id_type=pl.DeviceIdType.MESH,
        )

    def blk_copy(c, owner, bit, own=False):
        return pltpu.make_async_remote_copy(
            src_ref=teacher_hbm if own else block(c, owner), dst_ref=block(c, owner), send_sem=blk_send, recv_sem=blk_recv.at[c, owner],
            device_id=peer(0, bit), device_id_type=pl.DeviceIdType.MESH,
        )

    for i in range(1, nt):
        tok_copy(i, t).start()
    for bit in bits:
        blk_copy(t, b, bit, True).start()

    def hold_own(d):
        c = t ^ d
        tok_copy(0, c).wait_recv()
        for bit in bits:
            blk_copy(c, b, bit).start()

    def forward(d, lowest):
        c = t ^ d
        for h in range(1, nb):
            if (h & -h) != lowest:
                continue
            blk_copy(c, b ^ h, lowest).wait_recv()
            for bit in bits:
                if bit < lowest:
                    blk_copy(c, b ^ h, bit).start()

    for load in load_masks:
        load.wait()
    own_students, own_teachers = meta_values()
    meta[0][place(phases[0])] = jnp.concatenate(
        [jnp.broadcast_to(own_students, (1, 128)), jnp.broadcast_to(own_teachers, (1, 128))], axis=1
    )
    send_all(meta[0], meta_send.at[0], meta_recv.at[0], phases[0])

    def multiply(c, columns, first):
        part = lax.dot_general(
            x_ref[:, columns], all_t[c], (((1,), (1,)), ((), ())), preferred_element_type=jnp.float32
        )
        if first:
            s_ref[...] = part
        else:
            s_ref[...] += part

    aligned = fs % 128 == 0 and nt <= 8
    if aligned:
        for d in range(nt + len(bits)):
            if 0 < d < nt:
                hold_own(d)
            for k, bit in enumerate(bits):
                if 0 <= d - k - 1 < nt:
                    forward(d - k - 1, bit)
            done = d - len(bits)
            if 0 <= done < nt:
                if done == 0:
                    load_t.wait()
                    load_x.wait()
                c = t ^ done
                multiply(c, pl.ds(pl.multiple_of(c * fs, 128), fs), done == 0)
    else:
        def step(d, carry):
            hold_own(d)
            return carry

        lax.fori_loop(1, nt, step, 0)
        for bit in bits:
            def pass_on(d, carry, bit=bit):
                forward(d, bit)
                return carry

            lax.fori_loop(0, nt, pass_on, 0)
        load_t.wait()
        load_x.wait()
        for c in range(nt):
            multiply(c, pl.ds(c * fs, fs), c == 0)

    store_t = pltpu.make_async_copy(all_t, copied_t, out_sem.at[0])
    store_t.start()

    arrived(meta[0], meta_recv.at[0], phases[0])
    lane = lax.broadcasted_iota(jnp.int32, (1, m), 1)
    limit = jnp.zeros((1, m), jnp.float32)
    teacher_total = jnp.zeros((1, 1), jnp.float32)
    for j in range(nb):
        slot = t * nb + j if len(phases[0]) == 2 else j
        held = meta[0][slot][:, 128:129]
        teacher_total += held
        limit = jnp.where(lane // tb == j, held, limit)
    valid_teacher = (lane % tb).astype(jnp.float32) < limit
    log_teacher = jnp.where(valid_teacher, -jnp.log(teacher_total), NEG)
    student_total = jnp.sum(meta[0][...][:, :, 0:1], axis=0)
    if len(phases) == 2:
        meta[1][place(phases[1])] = jnp.broadcast_to(student_total, (1, 256))
        send_all(meta[1], meta_send.at[1], meta_recv.at[1], phases[1])
        arrived(meta[1], meta_recv.at[1], phases[1])
        student_total = jnp.sum(meta[1][...][:, :, 0:1], axis=0)
    log_count = jnp.log(student_total)

    def log_sum(values):
        top = jnp.max(values, axis=0)
        return top + jnp.log(jnp.sum(jnp.exp(values - top[None]), axis=0))

    terms = log_teacher
    for it in range(ITERS):
        top = jnp.full((8, m), -jnp.inf, jnp.float32)
        for r in range(0, rows, ROWS):
            s = s_ref[pl.ds(r, ROWS), :]
            if it == 0:
                s = s * scale
                s_ref[pl.ds(r, ROWS), :] = s
            row = s + terms
            high = jnp.max(row, axis=1, keepdims=True)
            lse = high + jnp.log(jnp.sum(jnp.exp(row - high), axis=1, keepdims=True))
            place_in = lax.broadcasted_iota(jnp.int32, (ROWS, 1), 0) + r
            real = place_in.astype(jnp.float32) < own_students
            column = s - lse + jnp.where(real, 0.0, NEG)
            c_ref[pl.ds(r, ROWS), :] = column
            top = jnp.maximum(top, jnp.max(column.reshape(ROWS // 8, 8, m), axis=0))
            if it == ITERS - 1:
                lse_ref[pl.ds(r, ROWS), :] = jnp.broadcast_to(lse, (ROWS, 128))
        top = jnp.max(top, axis=0, keepdims=True)
        total = jnp.zeros((8, m), jnp.float32)
        for r in range(0, rows, ROWS):
            grown = jnp.exp(c_ref[pl.ds(r, ROWS), :] - top)
            total += jnp.sum(grown.reshape(ROWS // 8, 8, m), axis=0)
        partial = top + jnp.log(jnp.sum(total, axis=0, keepdims=True))
        for p, axes in enumerate(phases):
            box = stats[p].at[it]
            box[place(axes)] = partial
            send_all(box, stat_send.at[p, it], stat_recv.at[p, it], axes)
            if it == ITERS - 1 and p == 0:
                store_c = pltpu.make_async_copy(c_ref, column_hbm, out_sem.at[1])
                store_c.start()
                potential_ref[...] = (-EPS) * jnp.transpose(lse_ref[...])[0:1, :]
            arrived(box, stat_recv.at[p, it], axes)
            partial = log_sum(box[...])
        terms = (log_count - partial) + log_teacher

    terms_ref[...] = terms
    wait_bytes(all_t.at[pl.ds(0, nt - 1), pl.ds(0, tb), :], tok_send)
    wait_bytes(all_t.at[:, pl.ds(0, (nb - 1) * tb), :], blk_send)
    for p, axes in enumerate(phases):
        arrived(meta[p], meta_send.at[p], axes)
        for it in range(ITERS):
            arrived(stats[p].at[it], stat_send.at[p, it], axes)
    store_t.wait()
    store_c.wait()


def average(
    nt, column_hbm, all_t_hbm, terms_hbm, potential_hbm, targets_hbm, potential_out,
    c_ref, t_ref, terms_ref, o_ref, in_sem, t_sem, out_sem,
):
    fs = t_ref.shape[2]
    loads = [
        pltpu.make_async_copy(terms_hbm, terms_ref, in_sem.at[0]),
        pltpu.make_async_copy(column_hbm, c_ref, in_sem.at[1]),
    ]
    blocks = [pltpu.make_async_copy(all_t_hbm.at[c], t_ref.at[c], t_sem.at[c]) for c in range(nt)]
    pass_on = pltpu.make_async_copy(potential_hbm, potential_out, in_sem.at[2])
    for load in loads + blocks + [pass_on]:
        load.start()
    for load in loads:
        load.wait()
    weights = jnp.exp(c_ref[...] + terms_ref[...]).astype(jnp.bfloat16)
    stores = []
    for c in range(nt):
        blocks[c].wait()
        part = pl.ds(c * fs, fs)
        o_ref[:, part] = jnp.dot(weights, t_ref[c], preferred_element_type=jnp.float32).astype(jnp.bfloat16)
        if fs % 128 == 0:
            stores.append(pltpu.make_async_copy(o_ref.at[:, part], targets_hbm.at[:, part], out_sem.at[c]))
            stores[-1].start()
    if not stores:
        stores.append(pltpu.make_async_copy(o_ref, targets_hbm, out_sem.at[0]))
        stores[-1].start()
    for store in stores + [pass_on]:
        store.wait()


def shards(nt, nb, student, teacher, student_mask, teacher_mask):
    rows, width = student.shape
    tb, fs = teacher.shape
    m = nb * tb
    phases = [("tok", "blk")] if nt * nb <= DIRECT else [("blk",), ("tok",)]
    sizes = [math.prod({"tok": nt, "blk": nb}[a] for a in axes) for axes in phases]
    vmem = pl.BlockSpec(memory_space=pltpu.VMEM)
    hbm = pl.BlockSpec(memory_space=pltpu.HBM)
    dma = pltpu.SemaphoreType.DMA
    column, whole_t, terms, potential = pl.pallas_call(
        functools.partial(kernel, nt, nb, phases, 1.0 / (math.sqrt(width) * EPS)),
        out_shape=(
            jax.ShapeDtypeStruct((rows, m), jnp.float32),
            jax.ShapeDtypeStruct((nt, m, fs), jnp.bfloat16),
            jax.ShapeDtypeStruct((1, m), jnp.float32),
            jax.ShapeDtypeStruct((1, rows), jnp.float32),
        ),
        in_specs=[hbm] * 4,
        out_specs=(hbm, hbm, vmem, vmem),
        scratch_shapes=[
            pltpu.VMEM((1, rows), jnp.int32),
            pltpu.VMEM((1, tb), jnp.int32),
            pltpu.VMEM((rows, width), jnp.bfloat16),
            pltpu.VMEM((nt, m, fs), jnp.bfloat16),
            pltpu.VMEM((rows, m), jnp.float32),
            pltpu.VMEM((rows, m), jnp.float32),
            pltpu.VMEM((rows, 128), jnp.float32),
            [pltpu.VMEM((size, 1, 256), jnp.float32) for size in sizes],
            [pltpu.VMEM((ITERS, size, 1, m), jnp.float32) for size in sizes],
            dma((4,)),
            dma((2,)),
            dma(()),
            dma((nt,)),
            dma(()),
            dma((nt, nb)),
            dma((2,)),
            dma((2,)),
            dma((2, ITERS)),
            dma((2, ITERS)),
        ],
        compiler_params=pltpu.CompilerParams(
            collective_id=0, has_side_effects=True, vmem_limit_bytes=60 * 2**20
        ),
        cost_estimate=pl.CostEstimate(
            flops=4 * rows * m * width, bytes_accessed=4 * rows * width + 2 * m * width, transcendentals=7 * rows * m
        ),
    )(student, teacher, student_mask.reshape(1, rows), teacher_mask.reshape(1, tb))
    targets, potential = pl.pallas_call(
        functools.partial(average, nt),
        out_shape=(
            jax.ShapeDtypeStruct((rows, width), jnp.bfloat16),
            jax.ShapeDtypeStruct((1, rows), jnp.float32),
        ),
        in_specs=[hbm] * 4,
        out_specs=(hbm, hbm),
        scratch_shapes=[
            pltpu.VMEM((rows, m), jnp.float32),
            pltpu.VMEM((nt, m, fs), jnp.bfloat16),
            pltpu.VMEM((1, m), jnp.float32),
            pltpu.VMEM((rows, width), jnp.bfloat16),
            dma((3,)),
            dma((nt,)),
            dma((nt,)),
        ],
        compiler_params=pltpu.CompilerParams(vmem_limit_bytes=60 * 2**20),
    )(column, whole_t, terms, potential)
    return targets, potential.reshape(rows)


def solution(mesh):
    in_specs = (
        P(("grp", "tok", "blk"), None),
        P(("grp", "blk"), "tok"),
        P(("grp", "tok", "blk")),
        P(("grp", "blk")),
    )
    out_specs = (P(("grp", "tok", "blk"), None), P(("grp", "tok", "blk")))
    body = functools.partial(shards, mesh.shape["tok"], mesh.shape["blk"])
    return jax.shard_map(body, mesh=mesh, in_specs=in_specs, out_specs=out_specs, check_vma=False)
```
